512 devices in a mesh: table: 32 (over y_hi, z), dp: 16 (over x, y_lo, core).
Axes of the slice: x: 4, y: 8 (y_hi: 4, y_lo: 2; y = y_hi * 2 + y_lo), z: 8, core: 2. Of those that a mesh axis runs over, the one named last changes fastest.
Arguments:
- features: bfloat16 [6144, 131072], P('dp', 'table'), may hold values from -6 to 6
- weight: bfloat16 [131072, 256], P(('table', 'dp')), may hold values from -0.015625 to 0.015625
- moment_one: float32 [131072, 256], P(('table', 'dp')), may hold values from -6 to 6
- moment_two: float32 [131072, 256], P(('table', 'dp')), may hold values from 1 to 10
- cotangent: bfloat16 [6144, 256], P('dp'), may hold values from -0.375 to 0.375
Outputs:
- hidden: bfloat16 [6144, 256], P(('dp', 'table'))
- new_moment_one: float32 [131072, 256], P(('table', 'dp'))
- new_moment_two: float32 [131072, 256], P(('table', 'dp'))
- direction: float32 [131072, 256], P(('table', 'dp'))
The draws below stay inside these ranges and needn't reach their ends.
All inputs are finite; a program needn't handle non-finite values.
Results may differ from the reference program's by a relative error of at most 0.0025.
Values may be sent and summed in bfloat16 or wider, within the bound.
A program may use at most 64 MiB of HBM per device.

```python
import math
import jax
import jax.numpy as jnp
from jax import lax

H = 256
TOK_DEV = 384
BATCH = 6144
INPUTS = 131072
N_DP = 16


def levels(key, dims, pieces, smallest, high):
    factor_of = 1.0
    for axis_at, parts in pieces:
        steps = jax.random.uniform(jax.random.fold_in(jax.random.fold_in(key, 6), axis_at), (parts,), jnp.float32, smallest / len(pieces), high / len(pieces))
        factor_of = factor_of * jnp.repeat(jnp.exp(steps), dims[axis_at] // parts).reshape((-1,) + (1,) * (len(dims) - 1 - axis_at))
    return factor_of


def noise(key, extent, scale, limit, shards=(), kind=jnp.bfloat16):
    loudness = levels(key, extent, shards, -0.22, 0.18) if shards else 1.0
    result = jax.random.normal(key, extent, jnp.float32) * scale * loudness
    return jnp.minimum(jnp.maximum(result, -limit), limit).astype(kind)


def setup_inputs(seed: int = 0) -> dict:
    key_of = jax.random.split(jax.random.key(seed), 6)
    features = noise(key_of[0], (BATCH, INPUTS), 1.0, 6.0, ((0, 16), (1, 32)))
    weight = noise(key_of[1], (INPUTS, H), INPUTS ** -0.5, 0.015625, ((0, 512),))
    moment_one = noise(key_of[2], (INPUTS, H), 1.0, 6.0, ((0, 512),), jnp.float32)
    moment_two = jnp.clip(jnp.exp(math.log(10.0) - 2.3025851 * jax.random.uniform(key_of[3], (INPUTS, H), jnp.float32) ** levels(key_of[3], (INPUTS, H), ((0, 512),), -0.2, 0.2)), 1.0, 10.0)
    cotangent = noise(key_of[4], (BATCH, H), (5 * (TOK_DEV * N_DP) ** -0.5), 0.375, ((0, 16),))
    return {"features": features, "weight": weight, "moment_one": moment_one, "moment_two": moment_two, "cotangent": cotangent}


bias_one = 0.99997343860111
bias_two = 0.63396765872677

def silu_slope(pre):
    sigma = jax.nn.sigmoid(pre)
    return sigma * (1.0 + pre * (1.0 - sigma))

def reference(features, weight, moment_one, moment_two, cotangent):
    pre = jnp.dot(features, weight, preferred_element_type=jnp.float32)
    hidden = jax.nn.silu(pre).astype(jnp.bfloat16)
    slope = (cotangent.astype(jnp.float32) * silu_slope(pre)).astype(jnp.bfloat16)
    inputs = features.shape[1]
    grouped_x = features.reshape(N_DP, TOK_DEV, inputs)
    grouped_s = slope.reshape(N_DP, TOK_DEV, H)

    def add_group(total, pair):
        partial_value = lax.dot_general(pair[0], pair[1], (((0,), (0,)), ((), ())), preferred_element_type=jnp.float32)
        return (total + partial_value, None)
    grad, unused = lax.scan(add_group, jnp.zeros((inputs, H), jnp.float32), (grouped_x, grouped_s))
    new_moment_one = 0.9 * moment_one + 0.1 * grad
    new_moment_two = 0.99 * moment_two + 0.01 * grad * grad
    direction = new_moment_one / bias_one / (jnp.sqrt(new_moment_two / bias_two) + 1e-08)
    return (hidden, new_moment_one, new_moment_two, direction)
```

```python
import jax
import jax.numpy as jnp
from jax import lax
from jax.experimental import pallas as pl
from jax.experimental.pallas import tpu as pltpu
from jax.sharding import PartitionSpec as P

bias_one = 0.99997343860111
bias_two = 0.63396765872677

NX, NY, NC = 4, 2, 2
NU, NZ = 4, 8
LANES = NX * NY
HALVES, COLS = 2, 128
ROWS, DEPTH = 384, 256
OWN = ROWS // (NU * NZ)
PACK = OWN * NU
ORDER = (5, 4, 3, 7, 2, 6, 1)
ZORDER = (4, 3, 5, 2, 6, 1, 7)
UORDER = (2, 1, 3)
MESH = pl.DeviceIdType.MESH


def silu_slope(pre):
    sigma = jax.nn.sigmoid(pre)
    return sigma * (1.0 + pre * (1.0 - sigma))


def kernel(
    x_hbm, w_hbm, cot_hbm, pre_out, grad_out,
    xv, wb, cv, cp, part, sb, zr, us, ur, sl, sg, gs, gr, gl, ls, lr,
    x_sem, cot_sem, own_sem,
    a_send, a_recv, f_send, f_recv,
    z_send, z_recv, u_send, u_recv, s_send, s_recv,
    g_send, g_recv, l_send, l_recv,
):
    table = lax.axis_index("table")
    dp = lax.axis_index("dp")
    u, z = table // NZ, table % NZ
    x, y, c = dp // (NY * NC), (dp // NC) % NY, dp % NC

    def lane(rel, sign, core):
        dx, dy = rel // NY, rel % NY
        px = (x + sign * dx + NX) % NX
        py = (y + dy) % NY
        return (px * NY + py) * NC + core

    def along_z(dz, sign):
        return u * NZ + (z + sign * dz + NZ) % NZ

    def along_u(du, sign):
        return ((u + sign * du + NU) % NU) * NZ + z

    other = 1 - c
    sibling = lane(0, 1, other)

    def to_dp(src, dst, send, recv, peer):
        return pltpu.make_async_remote_copy(
            src_ref=src, dst_ref=dst, send_sem=send, recv_sem=recv,
            device_id=(table, peer), device_id_type=MESH)

    def to_table(src, dst, send, recv, peer):
        return pltpu.make_async_remote_copy(
            src_ref=src, dst_ref=dst, send_sem=send, recv_sem=recv,
            device_id=(peer, dp), device_id_type=MESH)

    x_copy = pltpu.make_async_copy(x_hbm, xv, x_sem)
    x_copy.start()
    cot_copy = pltpu.make_async_copy(cot_hbm, cv, cot_sem)
    cot_copy.start()

    barrier = pltpu.get_barrier_semaphore()
    pl.semaphore_signal(barrier, inc=1, device_id=(table, sibling), device_id_type=MESH)
    for rel in ORDER:
        pl.semaphore_signal(barrier, inc=1, device_id=(table, lane(rel, 1, c)), device_id_type=MESH)
    for dz in ZORDER:
        pl.semaphore_signal(barrier, inc=1, device_id=(along_z(dz, 1), dp), device_id_type=MESH)
    for du in UORDER:
        pl.semaphore_signal(barrier, inc=1, device_id=(along_u(du, 1), dp), device_id_type=MESH)
    pl.semaphore_wait(barrier, 1 + len(ORDER) + len(ZORDER) + len(UORDER))

    def block(ref, h, at):
        return ref.at[h, at]

    def gather_copy(h, rel):
        return to_dp(w_hbm.at[:, pl.ds(h * COLS, COLS)], wb.at[h, dp],
                     a_send.at[h, rel], a_recv.at[h, rel], lane(rel, 1, c))

    def forward_copy(h, rel):
        src = lane(rel, -1, c)
        if rel == 0:
            return to_dp(w_hbm.at[:, pl.ds(h * COLS, COLS)], wb.at[h, dp],
                         f_send.at[h, 0], f_recv.at[h, 0], sibling)
        return to_dp(wb.at[h, src], wb.at[h, src], f_send.at[h, rel], f_recv.at[h, rel], sibling)

    def own_copy(h):
        return pltpu.make_async_copy(w_hbm.at[:, pl.ds(h * COLS, COLS)], wb.at[h, dp], own_sem.at[h])

    def gather_start(h):
        for rel in ORDER:
            gather_copy(h, rel).start()
        forward_copy(h, 0).start()
        own_copy(h).start()

    def add_block(h, src, first=False):
        columns = pl.ds(pl.multiple_of(src * DEPTH, DEPTH), DEPTH)
        product = jnp.dot(xv[:, columns], wb[h, src], preferred_element_type=jnp.float32)
        if first:
            part[h] = product
        else:
            part[h] += product

    def gather_finish(h):
        own_copy(h).wait()
        if h == 0:
            x_copy.wait()
        add_block(h, dp, True)
        for rel in ORDER[::-1]:
            src = lane(rel, -1, c)
            to_dp(wb.at[h, src], wb.at[h, src], a_send.at[h, rel], a_recv.at[h, rel], sibling).wait_recv()
            forward_copy(h, rel).start()
            add_block(h, src)
        for rel in (0,) + ORDER[::-1]:
            src = lane(rel, -1, other)
            to_dp(wb.at[h, src], wb.at[h, src], f_send.at[h, rel], f_recv.at[h, rel], sibling).wait_recv()
            add_block(h, src)

    def z_copy(h, dz):
        return to_table(sb.at[h, (z + dz) % NZ], zr.at[h, dz], z_send.at[h, dz], z_recv.at[h, dz],
                        along_z(dz, 1))

    def z_start(h):
        for at in range(NZ):
            for k in range(NU):
                sb[h, at, k * OWN:(k + 1) * OWN, :] = part[h, (k * NZ + at) * OWN:(k * NZ + at + 1) * OWN, :]
        for dz in ZORDER:
            z_copy(h, dz).start()

    def u_copy(h, du):
        return to_table(us.at[h], ur.at[h, du], u_send.at[h, du], u_recv.at[h, du], along_u(du, 1))

    def z_finish(h):
        total = sb[h, z]
        for dz in ZORDER[::-1]:
            z_copy(h, dz).wait_recv()
            total = total + zr[h, dz]
        us[h] = total
        for du in UORDER:
            u_copy(h, du).start()

    def s_copy(h, dz):
        return to_table(sl.at[h], sg.at[h, z], s_send.at[h, dz], s_recv.at[h, dz], along_z(dz, 1))

    def u_finish(h):
        pre = us[h]
        for du in UORDER[::-1]:
            u_copy(h, du).wait_recv()
            pre = pre + ur[h, du]
        here = slice(h * COLS, (h + 1) * COLS)
        slope = (cp[z, :, here] * silu_slope(pre)).astype(jnp.bfloat16)
        sl[h] = slope
        for dz in ZORDER:
            s_copy(h, dz).start()
        sg[h, z] = slope
        own = pre[0:OWN]
        for k in range(1, NU):
            own = jnp.where(u == k, pre[k * OWN:(k + 1) * OWN], own)
        pre_out[:, here] = own

    def spread(rows, cols):
        i = lax.broadcasted_iota(jnp.int32, (rows, cols), 0)
        j = lax.broadcasted_iota(jnp.int32, (rows, cols), 1)
        k, at, r = i // (NZ * OWN), (i // OWN) % NZ, i % OWN
        return (j == (at * NU + k) * OWN + r).astype(jnp.bfloat16)

    def g_copy(h, rel):
        return to_dp(gs.at[h, rel], gr.at[h, rel], g_send.at[h, rel], g_recv.at[h, rel], sibling)

    def l_copy(h, rel):
        return to_dp(ls.at[h, rel], lr.at[h, rel], l_send.at[h, rel], l_recv.at[h, rel], lane(rel, 1, c))

    def grad_block(slope_t, dst):
        columns = pl.ds(pl.multiple_of(dst * DEPTH, DEPTH), DEPTH)
        return jnp.dot(slope_t, xv[:, columns], preferred_element_type=jnp.float32)

    def grad_start(h):
        for dz in ZORDER[::-1]:
            src = (z + NZ - dz) % NZ
            to_table(sg.at[h, src], sg.at[h, src], s_send.at[h, dz], s_recv.at[h, dz], along_z(dz, 1)).wait_recv()
        packed = sg[h].reshape(ROWS, COLS)
        slope = jnp.dot(spread(ROWS, ROWS), packed, preferred_element_type=jnp.float32)
        slope_t = slope.T.astype(jnp.bfloat16)
        for rel in ORDER + (0,):
            gs[h, rel] = grad_block(slope_t, lane(rel, 1, other)).astype(gs.dtype)
            g_copy(h, rel).start()
        for rel in ORDER + (0,):
            mine = grad_block(slope_t, lane(rel, 1, c))
            g_copy(h, rel).wait_recv()
            mine = mine + gr[h, rel].astype(jnp.float32)
            if rel == 0:
                gl[h] = mine
            else:
                ls[h, rel] = mine.astype(jnp.bfloat16)
                l_copy(h, rel).start()

    def grad_finish(h):
        total = gl[h]
        for rel in ORDER[::-1]:
            l_copy(h, rel).wait_recv()
            total = total + lr[h, rel].astype(jnp.float32)
        grad_out[:, h * COLS:(h + 1) * COLS] = total.T

    gather_start(0)
    gather_start(1)
    cot_copy.wait()
    cot_f32 = cv[...].astype(jnp.float32)
    for at in range(NZ):
        for k in range(NU):
            cp[at, k * OWN:(k + 1) * OWN, :] = cot_f32[(k * NZ + at) * OWN:(k * NZ + at + 1) * OWN, :]
    gather_finish(0)
    z_start(0)
    gather_finish(1)
    z_start(1)
    z_finish(0)
    z_finish(1)
    u_finish(0)
    u_finish(1)
    grad_start(0)
    grad_start(1)
    grad_finish(0)
    grad_finish(1)

    for h in range(HALVES):
        for rel in ORDER:
            gather_copy(h, rel).wait_send()
            l_copy(h, rel).wait_send()
        for rel in (0,) + ORDER:
            forward_copy(h, rel).wait_send()
            g_copy(h, rel).wait_send()
        for dz in ZORDER:
            z_copy(h, dz).wait_send()
            s_copy(h, dz).wait_send()
        for du in UORDER:
            u_copy(h, du).wait_send()


def exchange(features, weight, cotangent):
    bf16, f32 = jnp.bfloat16, jnp.float32
    dma = pltpu.SemaphoreType.DMA
    vmem = pltpu.VMEM
    return pl.pallas_call(
        kernel,
        out_shape=(
            jax.ShapeDtypeStruct((OWN, HALVES * COLS), f32),
            jax.ShapeDtypeStruct((DEPTH, HALVES * COLS), f32),
        ),
        in_specs=[pl.BlockSpec(memory_space=pl.ANY)] * 3,
        out_specs=[pl.BlockSpec(memory_space=pltpu.VMEM)] * 2,
        scratch_shapes=[
            vmem((ROWS, NX * NY * NC * DEPTH), bf16),
            vmem((HALVES, NX * NY * NC, DEPTH, COLS), bf16),
            vmem((ROWS, HALVES * COLS), bf16),
            vmem((NZ, PACK, HALVES * COLS), f32),
            vmem((HALVES, ROWS, COLS), f32),
            vmem((HALVES, NZ, PACK, COLS), f32),
            vmem((HALVES, NZ, PACK, COLS), f32),
            vmem((HALVES, PACK, COLS), f32),
            vmem((HALVES, NU, PACK, COLS), f32),
            vmem((HALVES, PACK, COLS), bf16),
            vmem((HALVES, NZ, PACK, COLS), bf16),
            vmem((HALVES, LANES, COLS, DEPTH), f32),
            vmem((HALVES, LANES, COLS, DEPTH), f32),
            vmem((HALVES, COLS, DEPTH), f32),
            vmem((HALVES, LANES, COLS, DEPTH), bf16),
            vmem((HALVES, LANES, COLS, DEPTH), bf16),
            dma, dma, dma((HALVES,)),
            dma((HALVES, LANES)), dma((HALVES, LANES)), dma((HALVES, LANES)), dma((HALVES, LANES)),
            dma((HALVES, NZ)), dma((HALVES, NZ)), dma((HALVES, NU)), dma((HALVES, NU)),
            dma((HALVES, NZ)), dma((HALVES, NZ)),
            dma((HALVES, LANES)), dma((HALVES, LANES)), dma((HALVES, LANES)), dma((HALVES, LANES)),
        ],
        compiler_params=pltpu.CompilerParams(
            collective_id=0, has_side_effects=True, vmem_limit_bytes=48 * 1024 * 1024
        ),
    )(features, weight, cotangent)


def shards(features, weight, moment_one, moment_two, cotangent):
    pre, grad = exchange(features, weight, cotangent)
    hidden = jax.nn.silu(pre).astype(jnp.bfloat16)
    new_moment_one = 0.9 * moment_one + 0.1 * grad
    new_moment_two = 0.99 * moment_two + 0.01 * grad * grad
    direction = new_moment_one / bias_one / (jnp.sqrt(new_moment_two / bias_two) + 1e-08)
    return (hidden, new_moment_one, new_moment_two, direction)


def solution(mesh):
    return jax.shard_map(
        shards,
        mesh=mesh,
        in_specs=(
            P("dp", "table"),
            P(("table", "dp"), None),
            P(("table", "dp"), None),
            P(("table", "dp"), None),
            P("dp", None),
        ),
        out_specs=(
            P(("dp", "table"), None),
            P(("table", "dp"), None),
            P(("table", "dp"), None),
            P(("table", "dp"), None),
        ),
        check_vma=False,
    )
```

```python
import jax
import jax.numpy as jnp
from jax import lax
from jax.experimental import pallas as pl
from jax.experimental.pallas import tpu as pltpu
from jax.sharding import PartitionSpec as P

bias_one = 0.99997343860111
bias_two = 0.63396765872677

NX, NY, NC = 4, 2, 2
NU, NZ = 4, 8
LANES = NX * NY
PARTS, COLS = 4, 64
WIDE = 2 * COLS
ROWS, DEPTH = 384, 256
OWN = ROWS // (NU * NZ)
PACK = OWN * NU // 2
PADDED = 32
ORDER = (5, 4, 3, 7, 2, 6, 1)
ZORDER = (4, 3, 5, 2, 6, 1, 7)
UORDER = (2, 1, 3)
MESH = pl.DeviceIdType.MESH


def silu_slope(pre):
    sigma = jax.nn.sigmoid(pre)
    return sigma * (1.0 + pre * (1.0 - sigma))


def kernel(
    x_hbm, w_hbm, cot_hbm, pre_out, grad_out,
    xv, wv, wb, cv, cp, place, part, packed, own_part, sb, zr, us, ur, sl, sg, own_pre, gs, gr, gl, ls, lr, sums,
    x_sem, cot_sem, own_sem,
    a_send, a_recv, f_send, f_recv,
    z_send, z_recv, u_send, u_recv, s_send, s_recv,
    g_send, g_recv, l_send, l_recv,
):
    table = lax.axis_index("table")
    dp = lax.axis_index("dp")
    u, z = table // NZ, table % NZ
    x, y, c = dp // (NY * NC), (dp // NC) % NY, dp % NC

    def lane(rel, sign, core):
        dx, dy = rel // NY, rel % NY
        px = (x + sign * dx + NX) % NX
        py = (y + dy) % NY
        return (px * NY + py) * NC + core

    def along_z(dz, sign):
        return u * NZ + (z + sign * dz + NZ) % NZ

    def along_u(du, sign):
        return ((u + sign * du + NU) % NU) * NZ + z

    other = 1 - c
    sibling = lane(0, 1, other)

    def to_dp(src, dst, send, recv, peer):
        return pltpu.make_async_remote_copy(
            src_ref=src, dst_ref=dst, send_sem=send, recv_sem=recv,
            device_id=(table, peer), device_id_type=MESH)

    def to_table(src, dst, send, recv, peer):
        return pltpu.make_async_remote_copy(
            src_ref=src, dst_ref=dst, send_sem=send, recv_sem=recv,
            device_id=(peer, dp), device_id_type=MESH)

    w_copy = pltpu.make_async_copy(w_hbm, wv, own_sem)
    w_copy.start()
    x_copy = pltpu.make_async_copy(x_hbm, xv, x_sem)
    x_copy.start()
    cot_copy = pltpu.make_async_copy(cot_hbm, cv, cot_sem)
    cot_copy.start()

    barrier = pltpu.get_barrier_semaphore()
    pl.semaphore_signal(barrier, inc=1, device_id=(table, sibling), device_id_type=MESH)
    for rel in ORDER:
        pl.semaphore_signal(barrier, inc=1, device_id=(table, lane(rel, 1, c)), device_id_type=MESH)
    for dz in ZORDER:
        pl.semaphore_signal(barrier, inc=1, device_id=(along_z(dz, 1), dp), device_id_type=MESH)
    for du in UORDER:
        pl.semaphore_signal(barrier, inc=1, device_id=(along_u(du, 1), dp), device_id_type=MESH)

    def barrier_wait():
        pl.semaphore_wait(barrier, 1 + len(ORDER) + len(ZORDER) + len(UORDER))


    left = lax.broadcasted_iota(jnp.int32, (1, WIDE), 1) < COLS

    def turn(value):
        return pltpu.roll(value, COLS, 1)

    def pack(value, q):
        tile = value[:, q // 2 * WIDE:(q // 2 + 1) * WIDE]
        rows = tile.shape[0] // 2
        first, second = tile[:rows], tile[rows:]
        if q % 2 == 0:
            return jnp.where(left, first, turn(second))
        return jnp.where(left, turn(first), second)

    def gather_copy(q, rel):
        return to_dp(wb.at[q, dp], wb.at[q, dp], a_send.at[q, rel], a_recv.at[q, rel], lane(rel, 1, c))

    def forward_copy(q, rel):
        src = lane(rel, -1, c)
        return to_dp(wb.at[q, src], wb.at[q, src], f_send.at[q, rel], f_recv.at[q, rel], sibling)

    def gather_start(q):
        for rel in ORDER:
            gather_copy(q, rel).start()
        forward_copy(q, 0).start()

    def product(q, src):
        columns = pl.ds(pl.multiple_of(src * DEPTH, DEPTH), DEPTH)
        both = wb[q, src]
        swapped = turn(both.astype(jnp.float32)).astype(jnp.bfloat16)
        return jnp.dot(xv[:, columns], jnp.concatenate([both, swapped], axis=0),
                       preferred_element_type=jnp.float32)

    def gather_finish(q):
        for rel in ORDER[::-1]:
            src = lane(rel, -1, c)
            to_dp(wb.at[q, src], wb.at[q, src], a_send.at[q, rel], a_recv.at[q, rel], sibling).wait_recv()
            forward_copy(q, rel).start()
        part[...] = product(q, dp)
        for rel in ORDER[::-1]:
            part[...] += product(q, lane(rel, -1, c))
        for rel in (0,) + ORDER[::-1]:
            src = lane(rel, -1, other)
            to_dp(wb.at[q, src], wb.at[q, src], f_send.at[q, rel], f_recv.at[q, rel], sibling).wait_recv()
        for rel in (0,) + ORDER[::-1]:
            part[...] += product(q, lane(rel, -1, other))

    def z_copy(h, dz):
        return to_table(sb.at[h, (z + dz) % NZ], zr.at[h, dz], z_send.at[h, dz], z_recv.at[h, dz],
                        along_z(dz, 1))

    def z_start(h):
        half = ROWS // 2
        packed[...] = jnp.where(left, part[0:half], turn(part[half:ROWS]))
        for at in range(NZ):
            for k in range(NU // 2):
                sb[h, at, k * OWN:(k + 1) * OWN, :] = packed[(k * NZ + at) * OWN:(k * NZ + at + 1) * OWN, :]
        for dz in ZORDER:
            z_copy(h, dz).start()

    def u_copy(h, du):
        return to_table(us.at[h], ur.at[h, du], u_send.at[h, du], u_recv.at[h, du], along_u(du, 1))

    def z_finish(h):
        total = sb[h, z]
        for dz in ZORDER[::-1]:
            z_copy(h, dz).wait_recv()
            total = total + zr[h, dz]
        us[h] = total
        for du in UORDER:
            u_copy(h, du).start()

    def s_copy(h, dz):
        return to_table(sl.at[h], sg.at[h, z], s_send.at[h, dz], s_recv.at[h, dz], along_z(dz, 1))

    def u_finish(h):
        pre = us[h]
        for du in UORDER[::-1]:
            u_copy(h, du).wait_recv()
            pre = pre + ur[h, du]
        slope = cp[h, z] * silu_slope(pre)
        slope = jnp.concatenate([slope, jnp.zeros((PADDED - PACK, WIDE), jnp.float32)], axis=0)
        sl[h] = slope.astype(jnp.bfloat16)
        for dz in ZORDER:
            s_copy(h, dz).start()
        sg[h, z] = slope.astype(jnp.bfloat16)
        own = jnp.where(u % 2 == 0, pre[0:OWN], pre[OWN:2 * OWN])
        own_pre[h] = jnp.where(u // 2 == 0, own, turn(own))

    def spread():
        i = lax.broadcasted_iota(jnp.int32, (ROWS, NZ * PADDED), 0)
        j = lax.broadcasted_iota(jnp.int32, (ROWS, NZ * PADDED), 1)
        k, at, r = i // (NZ * OWN) % 2, (i // OWN) % NZ, i % OWN
        return (j == at * PADDED + k * OWN + r).astype(jnp.bfloat16)

    def g_copy(h, rel):
        return to_dp(gs.at[h, rel], gr.at[h, rel], g_send.at[h, rel], g_recv.at[h, rel], sibling)

    def l_copy(h, rel):
        return to_dp(ls.at[h, rel], lr.at[h, rel], l_send.at[h, rel], l_recv.at[h, rel], lane(rel, 1, c))

    def grad_block(slope_t, dst):
        columns = pl.ds(pl.multiple_of(dst * DEPTH, DEPTH), DEPTH)
        return jnp.dot(slope_t, xv[:, columns], preferred_element_type=jnp.float32)

    def grad_start(h):
        for dz in ZORDER[::-1]:
            src = (z + NZ - dz) % NZ
            to_table(sg.at[h, src], sg.at[h, src], s_send.at[h, dz], s_recv.at[h, dz], along_z(dz, 1)).wait_recv()
        slope = jnp.dot(place[...], sg[h].reshape(NZ * PADDED, WIDE), preferred_element_type=jnp.float32).T
        first = lax.broadcasted_iota(jnp.int32, (1, ROWS), 1) < ROWS // 2
        slope_t = jnp.where(first, slope[0:COLS], slope[COLS:WIDE]).astype(jnp.bfloat16)
        for group in (ORDER[:4], ORDER[4:] + (0,)):
            for rel in group:
                gs[h, rel] = grad_block(slope_t, lane(rel, 1, other)).astype(gs.dtype)
            for rel in group:
                g_copy(h, rel).start()
        for rel in ORDER + (0,):
            own_part[rel] = grad_block(slope_t, lane(rel, 1, c))
        for rel in ORDER + (0,):
            g_copy(h, rel).wait_recv()
            mine = own_part[rel] + gr[h, rel].astype(jnp.float32)
            if rel == 0:
                gl[h] = mine
            else:
                ls[h, rel] = mine.astype(jnp.bfloat16)
                l_copy(h, rel).start()

    def grad_finish(h):
        total = gl[h]
        for rel in ORDER[::-1]:
            l_copy(h, rel).wait_recv()
            total = total + lr[h, rel].astype(jnp.float32)
        sums[h % 2 * COLS:(h % 2 + 1) * COLS, :] = total
        if h % 2 == 1:
            grad_out[:, h // 2 * WIDE:(h // 2 + 1) * WIDE] = sums[...].T
            pre_out[:, h // 2 * WIDE:(h // 2 + 1) * WIDE] = jnp.where(left, own_pre[h - 1], turn(own_pre[h]))

    w_copy.wait()
    w_f32 = wv[...].astype(jnp.float32)
    for q in range(PARTS):
        wb[q, dp] = pack(w_f32, q).astype(jnp.bfloat16)
    barrier_wait()
    for q in range(PARTS):
        gather_start(q)
    place[...] = spread()
    cot_copy.wait()
    cot_f32 = cv[...].astype(jnp.float32)
    for q in range(PARTS):
        packed[...] = pack(cot_f32, q)
        for at in range(NZ):
            for k in range(NU // 2):
                cp[q, at, k * OWN:(k + 1) * OWN, :] = packed[(k * NZ + at) * OWN:(k * NZ + at + 1) * OWN, :]
    x_copy.wait()
    gather_finish(0)
    z_start(0)
    gather_finish(1)
    z_start(1)
    gather_finish(2)
    z_start(2)
    z_finish(0)
    gather_finish(3)
    z_start(3)
    z_finish(1)
    z_finish(2)
    u_finish(0)
    z_finish(3)
    u_finish(1)
    u_finish(2)
    grad_start(0)
    u_finish(3)
    grad_start(1)
    grad_start(2)
    grad_start(3)
    for q in range(PARTS):
        grad_finish(q)

    for h in range(PARTS):
        for rel in ORDER:
            gather_copy(h, rel).wait_send()
            l_copy(h, rel).wait_send()
        for rel in (0,) + ORDER:
            forward_copy(h, rel).wait_send()
            g_copy(h, rel).wait_send()
        for dz in ZORDER:
            z_copy(h, dz).wait_send()
            s_copy(h, dz).wait_send()
        for du in UORDER:
            u_copy(h, du).wait_send()


def exchange(features, weight, cotangent):
    bf16, f32 = jnp.bfloat16, jnp.float32
    dma = pltpu.SemaphoreType.DMA
    vmem = pltpu.VMEM
    return pl.pallas_call(
        kernel,
        out_shape=(
            jax.ShapeDtypeStruct((OWN, PARTS * COLS), f32),
            jax.ShapeDtypeStruct((DEPTH, PARTS * COLS), f32),
        ),
        in_specs=[pl.BlockSpec(memory_space=pltpu.HBM)] * 3,
        out_specs=[pl.BlockSpec(memory_space=pltpu.VMEM)] * 2,
        scratch_shapes=[
            vmem((ROWS, NX * NY * NC * DEPTH), bf16),
            vmem((DEPTH, PARTS * COLS), bf16),
            vmem((PARTS, NX * NY * NC, DEPTH // 2, WIDE), bf16),
            vmem((ROWS, PARTS * COLS), bf16),
            vmem((PARTS, NZ, PACK, WIDE), f32),
            vmem((ROWS, NZ * PADDED), bf16),
            vmem((ROWS, WIDE), f32),
            vmem((ROWS // 2, WIDE), f32),
            vmem((LANES, COLS, DEPTH), f32),
            vmem((PARTS, NZ, PACK, WIDE), f32),
            vmem((PARTS, NZ, PACK, WIDE), f32),
            vmem((PARTS, PACK, WIDE), f32),
            vmem((PARTS, NU, PACK, WIDE), f32),
            vmem((PARTS, PADDED, WIDE), bf16),
            vmem((PARTS, NZ, PADDED, WIDE), bf16),
            vmem((PARTS, OWN, WIDE), f32),
            vmem((PARTS, LANES, COLS, DEPTH), bf16),
            vmem((PARTS, LANES, COLS, DEPTH), bf16),
            vmem((PARTS, COLS, DEPTH), f32),
            vmem((PARTS, LANES, COLS, DEPTH), bf16),
            vmem((PARTS, LANES, COLS, DEPTH), bf16),
            vmem((WIDE, DEPTH), f32),
            dma, dma, dma,
            dma((PARTS, LANES)), dma((PARTS, LANES)), dma((PARTS, LANES)), dma((PARTS, LANES)),
            dma((PARTS, NZ)), dma((PARTS, NZ)), dma((PARTS, NU)), dma((PARTS, NU)),
            dma((PARTS, NZ)), dma((PARTS, NZ)),
            dma((PARTS, LANES)), dma((PARTS, LANES)), dma((PARTS, LANES)), dma((PARTS, LANES)),
        ],
        compiler_params=pltpu.CompilerParams(
            collective_id=0, has_side_effects=True, vmem_limit_bytes=48 * 1024 * 1024
        ),
    )(*(pltpu.with_memory_space_constraint(a, pltpu.HBM) for a in (features, weight, cotangent)))


def shards(features, weight, moment_one, moment_two, cotangent):
    pre, grad = exchange(features, weight, cotangent)
    hidden = jax.nn.silu(pre).astype(jnp.bfloat16)
    new_moment_one = 0.9 * moment_one + 0.1 * grad
    new_moment_two = 0.99 * moment_two + 0.01 * grad * grad
    direction = new_moment_one / bias_one / (jnp.sqrt(new_moment_two / bias_two) + 1e-08)
    return (hidden, new_moment_one, new_moment_two, direction)


def solution(mesh):
    return jax.shard_map(
        shards,
        mesh=mesh,
        in_specs=(
            P("dp", "table"),
            P(("table", "dp"), None),
            P(("table", "dp"), None),
            P(("table", "dp"), None),
            P("dp", None),
        ),
        out_specs=(
            P(("dp", "table"), None),
            P(("table", "dp"), None),
            P(("table", "dp"), None),
            P(("table", "dp"), None),
        ),
        check_vma=False,
    )
```

```python
import jax
import jax.numpy as jnp
from jax import lax
from jax.experimental import pallas as pl
from jax.experimental.pallas import tpu as pltpu
from jax.sharding import PartitionSpec as P

bias_one = 0.99997343860111
bias_two = 0.63396765872677

NX, NY, NC = 4, 2, 2
NU, NZ = 4, 8
LANES = NX * NY
PARTS, COLS = 4, 64
WIDE = 2 * COLS
ROWS, DEPTH = 384, 256
OWN = ROWS // (NU * NZ)
PACK = OWN * NU // 2
PADDED = 32
ORDER = (5, 4, 3, 7, 2, 6, 1)
BOTH = 2 * ROWS
ZORDER = (4, 3, 5, 2, 6, 1, 7)
UORDER = (2, 1, 3)
MESH = pl.DeviceIdType.MESH


def silu_slope(pre):
    sigma = jax.nn.sigmoid(pre)
    return sigma * (1.0 + pre * (1.0 - sigma))


def kernel(
    x_hbm, w_hbm, cot_hbm, pre_out, grad_out,
    xv, wv, wb, cv, cp, place, part, packed, pair_out, pair_in, sb, zr, us, ur, sl, sg, own_pre, mine, theirs, gl, ls, lr, sums,
    x_sem, cot_sem, own_sem, swap_send, swap_recv,
    a_send, a_recv, pair_send, pair_recv,
    z_send, z_recv, u_send, u_recv, s_send, s_recv,
    g_send, g_recv, l_send, l_recv,
):
    table = lax.axis_index("table")
    dp = lax.axis_index("dp")
    u, z = table // NZ, table % NZ
    x, y, c = dp // (NY * NC), (dp // NC) % NY, dp % NC

    def chip_at(rel, sign):
        return (x + sign * (rel // NY) + NX) % NX * NY + (y + rel % NY) % NY

    def lane(rel, sign, core):
        dx, dy = rel // NY, rel % NY
        px = (x + sign * dx + NX) % NX
        py = (y + dy) % NY
        return (px * NY + py) * NC + core

    def along_z(dz, sign):
        return u * NZ + (z + sign * dz + NZ) % NZ

    def along_u(du, sign):
        return ((u + sign * du + NU) % NU) * NZ + z

    other = 1 - c
    sibling = lane(0, 1, other)

    def to_dp(src, dst, send, recv, peer):
        return pltpu.make_async_remote_copy(
            src_ref=src, dst_ref=dst, send_sem=send, recv_sem=recv,
            device_id=(table, peer), device_id_type=MESH)

    def to_table(src, dst, send, recv, peer):
        return pltpu.make_async_remote_copy(
            src_ref=src, dst_ref=dst, send_sem=send, recv_sem=recv,
            device_id=(peer, dp), device_id_type=MESH)

    w_copy = pltpu.make_async_copy(w_hbm, wv, own_sem)
    w_copy.start()

    def x_copy(k):
        columns = pl.ds(pl.multiple_of((k * NC + c) * DEPTH, DEPTH), DEPTH)
        return pltpu.make_async_copy(x_hbm.at[:, columns], xv.at[k, pl.ds(0, ROWS)], x_sem.at[k])

    def x_swap(k):
        columns = pl.ds(pl.multiple_of((k * NC + other) * DEPTH, DEPTH), DEPTH)
        return to_dp(x_hbm.at[:, columns], xv.at[k, pl.ds(ROWS, ROWS)], swap_send.at[k], swap_recv.at[k], sibling)

    cot_copy = pltpu.make_async_copy(cot_hbm, cv, cot_sem)
    cot_copy.start()

    barrier = pltpu.get_barrier_semaphore()
    pl.semaphore_signal(barrier, inc=1, device_id=(table, sibling), device_id_type=MESH)
    for rel in ORDER:
        pl.semaphore_signal(barrier, inc=1, device_id=(table, lane(rel, 1, c)), device_id_type=MESH)
    for dz in ZORDER:
        pl.semaphore_signal(barrier, inc=1, device_id=(along_z(dz, 1), dp), device_id_type=MESH)
    for du in UORDER:
        pl.semaphore_signal(barrier, inc=1, device_id=(along_u(du, 1), dp), device_id_type=MESH)

    def barrier_wait():
        pl.semaphore_wait(barrier, 1 + len(ORDER) + len(ZORDER) + len(UORDER))


    left = lax.broadcasted_iota(jnp.int32, (1, WIDE), 1) < COLS

    def turn(value):
        return pltpu.roll(value, COLS, 1)

    def pack(value, q):
        tile = value[:, q // 2 * WIDE:(q // 2 + 1) * WIDE]
        rows = tile.shape[0] // 2
        first, second = tile[:rows], tile[rows:]
        if q % 2 == 0:
            return jnp.where(left, first, turn(second))
        return jnp.where(left, turn(first), second)

    def gather_copy(q, rel):
        return to_dp(wb.at[q, chip_at(0, 1)], wb.at[q, chip_at(0, 1)], a_send.at[q, rel], a_recv.at[q, rel], lane(rel, 1, c))

    def gather_start(q):
        for rel in ORDER:
            gather_copy(q, rel).start()

    def product(q, chip):
        block = wb[q, chip]
        swapped = turn(block.astype(jnp.float32)).astype(jnp.bfloat16)
        return jnp.dot(xv[chip], jnp.concatenate([block, swapped], axis=0), preferred_element_type=jnp.float32)

    def pair_copy(q):
        return to_dp(pair_out.at[q], pair_in.at[q], pair_send.at[q], pair_recv.at[q], sibling)

    def two_groups(rows):
        half = ROWS // 2
        return jnp.where(left, part[rows:rows + half], turn(part[rows + half:rows + ROWS]))

    def gather_finish(q):
        for group in (ORDER[:4], ORDER[4:]):
            for rel in group:
                src = chip_at(rel, -1)
                to_dp(wb.at[q, src], wb.at[q, src], a_send.at[q, rel], a_recv.at[q, rel], sibling).wait_recv()
            if group == ORDER[:4]:
                part[...] = product(q, chip_at(0, 1))
            elif q + 2 < PARTS:
                gather_start(q + 2)
            for rel in group:
                part[...] += product(q, chip_at(rel, -1))
        pair_out[q] = two_groups(ROWS)
        pair_copy(q).start()
        packed[q] = two_groups(0)

    def z_copy(h, dz):
        return to_table(sb.at[h, (z + dz) % NZ], zr.at[h, dz], z_send.at[h, dz], z_recv.at[h, dz],
                        along_z(dz, 1))

    def z_start(h):
        pair_copy(h).wait_recv()
        packed[h] += pair_in[h]
        for at in range(NZ):
            for k in range(NU // 2):
                sb[h, at, k * OWN:(k + 1) * OWN, :] = packed[h, (k * NZ + at) * OWN:(k * NZ + at + 1) * OWN, :]
        for dz in ZORDER:
            z_copy(h, dz).start()

    def u_copy(h, du):
        return to_table(us.at[h], ur.at[h, du], u_send.at[h, du], u_recv.at[h, du], along_u(du, 1))

    def z_finish(h):
        total = sb[h, z]
        for dz in ZORDER[::-1]:
            z_copy(h, dz).wait_recv()
            total = total + zr[h, dz]
        us[h] = total
        for du in UORDER:
            u_copy(h, du).start()

    def s_copy(h, dz):
        return to_table(sl.at[h], sg.at[h, z], s_send.at[h, dz], s_recv.at[h, dz], along_z(dz, 1))

    def u_finish(h):
        pre = us[h]
        for du in UORDER[::-1]:
            u_copy(h, du).wait_recv()
            pre = pre + ur[h, du]
        slope = cp[h, z] * silu_slope(pre)
        slope = jnp.concatenate([slope, jnp.zeros((PADDED - PACK, WIDE), jnp.float32)], axis=0)
        sl[h] = slope.astype(jnp.bfloat16)
        for dz in ZORDER:
            s_copy(h, dz).start()
        sg[h, z] = slope.astype(jnp.bfloat16)
        own = jnp.where(u % 2 == 0, pre[0:OWN], pre[OWN:2 * OWN])
        own_pre[h] = jnp.where(u // 2 == 0, own, turn(own))

    def spread():
        i = lax.broadcasted_iota(jnp.int32, (ROWS, NZ * PADDED), 0)
        j = lax.broadcasted_iota(jnp.int32, (ROWS, NZ * PADDED), 1)
        k, at, r = i // (NZ * OWN) % 2, (i // OWN) % NZ, i % OWN
        return (j == at * PADDED + k * OWN + r).astype(jnp.bfloat16)

    def g_copy(h):
        return to_dp(mine.at[h], theirs.at[h], g_send.at[h], g_recv.at[h], sibling)

    def l_copy(h, rel):
        return to_dp(ls.at[h, rel], lr.at[h, rel], l_send.at[h, rel], l_recv.at[h, rel], lane(rel, 1, c))

    def grad_start(h):
        for dz in ZORDER[::-1]:
            src = (z + NZ - dz) % NZ
            to_table(sg.at[h, src], sg.at[h, src], s_send.at[h, dz], s_recv.at[h, dz], along_z(dz, 1)).wait_recv()
        slope = jnp.dot(place[...], sg[h].reshape(NZ * PADDED, WIDE), preferred_element_type=jnp.float32).T
        first = lax.broadcasted_iota(jnp.int32, (1, ROWS), 1) < ROWS // 2
        mine[h] = jnp.where(first, slope[0:COLS], slope[COLS:WIDE]).astype(jnp.bfloat16)
        g_copy(h).start()

    def grad_send(h):
        g_copy(h).wait_recv()
        slope_t = jnp.concatenate([mine[h], theirs[h]], axis=1)
        for group in ((5, 4), (3, 7), (2, 6), (1, 0)):
            for rel in group:
                block = jnp.dot(slope_t, xv[chip_at(rel, 1)], preferred_element_type=jnp.float32)
                if rel == 0:
                    gl[h] = block
                else:
                    ls[h, rel] = block.astype(jnp.bfloat16)
            for rel in group:
                if rel != 0:
                    l_copy(h, rel).start()

    def grad_finish(h):
        total = gl[h]
        for rel in ORDER[::-1]:
            l_copy(h, rel).wait_recv()
            total = total + lr[h, rel].astype(jnp.float32)
        sums[h % 2 * COLS:(h % 2 + 1) * COLS, :] = total
        if h % 2 == 1:
            grad_out[:, h // 2 * WIDE:(h // 2 + 1) * WIDE] = sums[...].T
            pre_out[:, h // 2 * WIDE:(h // 2 + 1) * WIDE] = jnp.where(left, own_pre[h - 1], turn(own_pre[h]))

    for k in range(LANES):
        x_copy(k).start()
    w_copy.wait()
    w_f32 = wv[...].astype(jnp.float32)
    for q in range(PARTS):
        wb[q, chip_at(0, 1)] = pack(w_f32, q).astype(jnp.bfloat16)
    barrier_wait()
    gather_start(0)
    for k in range(LANES):
        x_swap(k).start()
    for q in range(1, 2):
        gather_start(q)
    place[...] = spread()
    cot_copy.wait()
    cot_f32 = cv[...].astype(jnp.float32)
    for q in range(PARTS):
        packed[q] = pack(cot_f32, q)
        for at in range(NZ):
            for k in range(NU // 2):
                cp[q, at, k * OWN:(k + 1) * OWN, :] = packed[q, (k * NZ + at) * OWN:(k * NZ + at + 1) * OWN, :]
    for k in range(LANES):
        x_copy(k).wait()
        x_swap(k).wait_recv()
    gather_finish(0)
    z_start(0)
    gather_finish(1)
    z_start(1)
    gather_finish(2)
    z_start(2)
    z_finish(0)
    gather_finish(3)
    z_start(3)
    z_finish(1)
    u_finish(0)
    z_finish(2)
    u_finish(1)
    z_finish(3)
    grad_start(0)
    u_finish(2)
    grad_send(0)
    grad_start(1)
    grad_send(1)
    u_finish(3)
    grad_start(2)
    grad_send(2)
    grad_finish(0)
    grad_start(3)
    grad_finish(1)
    grad_send(3)
    grad_finish(2)
    for k in range(LANES):
        x_swap(k).wait_send()
    for h in range(PARTS):
        for rel in ORDER:
            gather_copy(h, rel).wait_send()
            if h < PARTS - 1:
                l_copy(h, rel).wait_send()
        pair_copy(h).wait_send()
        g_copy(h).wait_send()
        for dz in ZORDER:
            z_copy(h, dz).wait_send()
            s_copy(h, dz).wait_send()
        for du in UORDER:
            u_copy(h, du).wait_send()
    grad_finish(3)

    for rel in ORDER:
        l_copy(PARTS - 1, rel).wait_send()


def exchange(features, weight, cotangent):
    bf16, f32 = jnp.bfloat16, jnp.float32
    dma = pltpu.SemaphoreType.DMA
    vmem = pltpu.VMEM
    return pl.pallas_call(
        kernel,
        out_shape=(
            jax.ShapeDtypeStruct((OWN, PARTS * COLS), f32),
            jax.ShapeDtypeStruct((DEPTH, PARTS * COLS), f32),
        ),
        in_specs=[pl.BlockSpec(memory_space=pltpu.HBM)] * 3,
        out_specs=[pl.BlockSpec(memory_space=pltpu.VMEM)] * 2,
        scratch_shapes=[
            vmem((LANES, BOTH, DEPTH), bf16),
            vmem((DEPTH, PARTS * COLS), bf16),
            vmem((PARTS, LANES, DEPTH // 2, WIDE), bf16),
            vmem((ROWS, PARTS * COLS), bf16),
            vmem((PARTS, NZ, PACK, WIDE), f32),
            vmem((ROWS, NZ * PADDED), bf16),
            vmem((BOTH, WIDE), f32),
            vmem((PARTS, ROWS // 2, WIDE), f32),
            vmem((PARTS, ROWS // 2, WIDE), f32),
            vmem((PARTS, ROWS // 2, WIDE), f32),
            vmem((PARTS, NZ, PACK, WIDE), f32),
            vmem((PARTS, NZ, PACK, WIDE), f32),
            vmem((PARTS, PACK, WIDE), f32),
            vmem((PARTS, NU, PACK, WIDE), f32),
            vmem((PARTS, PADDED, WIDE), bf16),
            vmem((PARTS, NZ, PADDED, WIDE), bf16),
            vmem((PARTS, OWN, WIDE), f32),
            vmem((PARTS, COLS, ROWS), bf16),
            vmem((PARTS, COLS, ROWS), bf16),
            vmem((PARTS, COLS, DEPTH), f32),
            vmem((PARTS, LANES, COLS, DEPTH), bf16),
            vmem((PARTS, LANES, COLS, DEPTH), bf16),
            vmem((WIDE, DEPTH), f32),
            dma((LANES,)), dma, dma, dma((LANES,)), dma((LANES,)),
            dma((PARTS, LANES)), dma((PARTS, LANES)), dma((PARTS,)), dma((PARTS,)),
            dma((PARTS, NZ)), dma((PARTS, NZ)), dma((PARTS, NU)), dma((PARTS, NU)),
            dma((PARTS, NZ)), dma((PARTS, NZ)),
            dma((PARTS,)), dma((PARTS,)), dma((PARTS, LANES)), dma((PARTS, LANES)),
        ],
        compiler_params=pltpu.CompilerParams(
            collective_id=0, has_side_effects=True, vmem_limit_bytes=48 * 1024 * 1024
        ),
    )(*(pltpu.with_memory_space_constraint(a, pltpu.HBM) for a in (features, weight, cotangent)))


def shards(features, weight, moment_one, moment_two, cotangent):
    pre, grad = exchange(features, weight, cotangent)
    hidden = jax.nn.silu(pre).astype(jnp.bfloat16)
    new_moment_one = 0.9 * moment_one + 0.1 * grad
    new_moment_two = 0.99 * moment_two + 0.01 * grad * grad
    direction = new_moment_one / bias_one / (jnp.sqrt(new_moment_two / bias_two) + 1e-08)
    return (hidden, new_moment_one, new_moment_two, direction)


def solution(mesh):
    return jax.shard_map(
        shards,
        mesh=mesh,
        in_specs=(
            P("dp", "table"),
            P(("table", "dp"), None),
            P(("table", "dp"), None),
            P(("table", "dp"), None),
            P("dp", None),
        ),
        out_specs=(
            P(("dp", "table"), None),
            P(("table", "dp"), None),
            P(("table", "dp"), None),
            P(("table", "dp"), None),
        ),
        check_vma=False,
    )
```
